32 devices in a mesh: xy: 16 (over z, x, core), gz: 2 (over y).
Axes of the slice: x: 2, y: 2, z: 4, core: 2. Of those that a mesh axis runs over, the one named last changes fastest.
Arguments:
- field_tiles: bfloat16 [16, 128, 128, 256], P('xy', None, None, 'gz'), may hold values from -6 to 6
- core_x: bfloat16 [512, 192], replicated, may hold values from -0.25 to 0.25
- core_y: bfloat16 [512, 192], replicated, may hold values from -0.25 to 0.25
- core_z: bfloat16 [256, 192], P('gz'), may hold values from -0.375 to 0.375
- x_second: bfloat16 [512, 96], replicated, may hold values from -0.25 to 0.25
- x_third: bfloat16 [512, 96], replicated, may hold values from -0.25 to 0.25
- y_first: bfloat16 [512, 96], replicated, may hold values from -0.25 to 0.25
- y_third: bfloat16 [512, 96], replicated, may hold values from -0.25 to 0.25
- z_first: bfloat16 [256, 96], P('gz'), may hold values from -0.375 to 0.375
- z_second: bfloat16 [256, 96], P('gz'), may hold values from -0.375 to 0.375
Outputs:
- mode_one: float32 [512, 96], P(('xy', 'gz'))
- mode_two: float32 [512, 96], P(('xy', 'gz'))
- mode_three: float32 [96, 256], P('xy', 'gz')
- core_sketch: float32 [192, 192, 192], P('xy', None, 'gz')
The draws below stay inside these ranges and needn't reach their ends.
All inputs are finite; a program needn't handle non-finite values.
Results may differ from the reference program's by a relative error of at most 0.007.
Values may be sent and summed in bfloat16 or wider, within the bound.
No kernel may reach another device: no remote copies, remote signals or barrier semaphores. Data moves between devices by JAX's collectives and lax.ppermute only.
A program may use at most 128 MiB of HBM per device.

```python
import jax
import jax.numpy as jnp
from jax import lax

K = 96
S = 192
TX = 128
TY = 128
NX = 512
NY = 512
NZ = 256
N_XY = 16


def block_scale(rng, extent, pieces, low, largest):
    factor_of = 1.0
    for dim, shards_of in pieces:
        steps = jax.random.uniform(jax.random.fold_in(jax.random.fold_in(rng, 6), dim), (shards_of,), jnp.float32, low / len(pieces), largest / len(pieces))
        factor_of = factor_of * jnp.repeat(jnp.exp(steps), extent[dim] // shards_of).reshape((-1,) + (1,) * (len(extent) - 1 - dim))
    return factor_of


def scatter_about(key, extent, spread, reach, cuts=(), kind=jnp.bfloat16):
    result = spread * jax.random.normal(key, extent, jnp.float32)
    if cuts:
        result = result * block_scale(key, extent, cuts, -0.22, 0.18)
    return jnp.clip(result, -reach, reach).astype(kind)


def setup_inputs(seed: int = 0) -> dict:
    streams_of = jax.random.split(jax.random.key(seed), 11)
    return {
        "field_tiles": scatter_about(streams_of[0], (N_XY, TX, TY, NZ), 1.0, 6.0, ((0, 16), (3, 2))),
        "core_x": scatter_about(streams_of[1], (NX, S), NX ** -0.5, 0.25),
        "core_y": scatter_about(streams_of[2], (NY, S), NY ** -0.5, 0.25),
        "core_z": scatter_about(streams_of[3], (NZ, S), NZ ** -0.5, 0.375, ((0, 2),)),
        "x_second": scatter_about(streams_of[4], (NX, K), NX ** -0.5, 0.25),
        "x_third": scatter_about(streams_of[5], (NX, K), NX ** -0.5, 0.25),
        "y_first": scatter_about(streams_of[6], (NY, K), NY ** -0.5, 0.25),
        "y_third": scatter_about(streams_of[7], (NY, K), NY ** -0.5, 0.25),
        "z_first": scatter_about(streams_of[8], (NZ, K), NZ ** -0.5, 0.375, ((0, 2),)),
        "z_second": scatter_about(streams_of[9], (NZ, K), NZ ** -0.5, 0.375, ((0, 2),)),
    }


def row_slice(matrix, offset, length):
    return lax.dynamic_slice_in_dim(matrix, offset, length, 0).astype(jnp.float32)


def reference(field_tiles, core_x, core_y, core_z, x_second, x_third, y_first, y_third, z_first, z_second):
    column_tiles = N_XY // 4
    z_pair = jnp.concatenate([z_first, z_second], axis=1).astype(jnp.float32)

    def one_tile(totals, tile_index):
        first_part, second_part, third_part, plane_sum = totals
        block_data = lax.dynamic_index_in_dim(field_tiles, tile_index, 0, keepdims=False).astype(jnp.float32)
        x_offset = ((tile_index // column_tiles) * TX).astype(jnp.int32)
        y_offset = ((tile_index % column_tiles) * TY).astype(jnp.int32)
        paired = jnp.einsum('abz,zk->abk', block_data, z_pair)
        g_one = jnp.sum(paired[:, :, :K] * row_slice(y_first, y_offset, TY)[None], axis=1)
        g_two = jnp.sum(paired[:, :, K:] * row_slice(x_second, x_offset, TX)[:, None], axis=0)
        across = jnp.einsum('abz,ak->bkz', block_data, row_slice(x_third, x_offset, TX))
        g_three = jnp.sum(across * row_slice(y_third, y_offset, TY)[:, :, None], axis=0)
        first_part = lax.dynamic_update_slice_in_dim(
            first_part, lax.dynamic_slice_in_dim(first_part, x_offset, TX, 0) + g_one, x_offset, 0)
        second_part = lax.dynamic_update_slice_in_dim(
            second_part, lax.dynamic_slice_in_dim(second_part, y_offset, TY, 0) + g_two, y_offset, 0)
        third_part = third_part + g_three
        lowered = jnp.einsum('abz,ap->pbz', block_data, row_slice(core_x, x_offset, TX)).astype(jnp.bfloat16)
        plane_sum = plane_sum + jnp.einsum('pbz,bq->pqz', lowered.astype(jnp.float32), row_slice(core_y, y_offset, TY))
        return (first_part, second_part, third_part, plane_sum), None

    start_totals = (jnp.zeros((NX, K), jnp.float32), jnp.zeros((NY, K), jnp.float32),
                    jnp.zeros((K, NZ), jnp.float32), jnp.zeros((S, S, NZ), jnp.float32))
    totals, _ = lax.scan(one_tile, start_totals, jnp.arange(N_XY, dtype=jnp.int32))
    mode_one, mode_two, mode_three, plane_sum = totals
    core_sketch = jnp.einsum('pqz,zr->pqr', plane_sum, core_z.astype(jnp.float32), precision=lax.Precision.HIGHEST)
    return mode_one, mode_two, mode_three, core_sketch
```

```python
import functools

import jax
import jax.numpy as jnp
from jax import lax
from jax.experimental import pallas as pl
from jax.experimental.pallas import tpu as pltpu
from jax.sharding import PartitionSpec as P

TX = 128
TY = 128
LANES = 128
REGIONS = 8
ROWS = 32
UNIT = 8
PLAN = (1, 1, 1, 1, 1, 1)
PAIR_PLAN = (1, 1, 1, 1, 1, 1)
RIDING = 1
EARLY = 3
WAIT = 0
LAG = 3.1
PACK = 4
F32 = jnp.float32
BF16 = jnp.bfloat16


def dot(a, b):
    return jnp.dot(a, b, preferred_element_type=F32)


def cut(matrix, offset, length, axis):
    return lax.dynamic_slice_in_dim(matrix, offset, length, axis)


def modes_kernel(
    tile, low, high, z_first, z_second, y_one, x_two, y_three, x_three, one, two, three, z_pair, ones, twos, x_parts
):
    del tile
    step, rows = pl.program_id(0), 2 * low.shape[0]
    k = y_three.shape[0]

    @pl.when(step == 0)
    def _():
        two[...] = jnp.zeros_like(two)
        three[...] = jnp.zeros_like(three)
        for ref in (z_pair, ones, twos):
            ref[...] = jnp.zeros_like(ref)
        z_pair[:, :k] = z_first[...].astype(F32).T.astype(BF16)
        z_pair[:, LANES : LANES + k] = z_second[...].astype(F32).T.astype(BF16)
        ones[:, :k] = y_one[...].astype(F32).T
        twos[:, :k] = x_two[...].astype(F32).T
        for n in range(x_parts.shape[0]):
            x_parts[n] = x_three[...].astype(F32)[:, n * rows : (n + 1) * rows]

    sum_two = jnp.zeros(two.shape, F32)
    sum_three = jnp.zeros(three.shape, F32)
    for i in range(rows):
        plane = (low, high)[i * 2 // rows][i % low.shape[0]]
        paired = dot(plane, z_pair[...])
        one[i : i + 1, :] = jnp.sum(paired[:, :LANES] * ones[...], axis=0, keepdims=True)
        sum_two += paired[:, LANES:] * twos[pl.ds(step * rows + i, 1), :]
        sum_three += dot(y_three[...], plane) * x_parts[step, :, i : i + 1]
    two[...] += sum_two
    three[...] += sum_three


def modes(tile, field, z_first, z_second, y_first, x_second, y_third, x_third):
    tx, ty, nz = field.shape
    k = z_first.shape[1]
    steps = tx // ROWS
    whole = lambda *shape: pl.BlockSpec(shape, lambda i, tile: (0,) * len(shape))
    row = pl.BlockSpec((k, tx), lambda i, tile: (0, tile[0]))
    column = pl.BlockSpec((k, ty), lambda i, tile: (0, tile[1]))
    return pl.pallas_call(
        modes_kernel,
        grid_spec=pltpu.PrefetchScalarGridSpec(
            num_scalar_prefetch=1,
            grid=(steps,),
            in_specs=[
                pl.BlockSpec((ROWS // 2, ty, nz), lambda i, tile: (2 * i, 0, 0)),
                pl.BlockSpec((ROWS // 2, ty, nz), lambda i, tile: (2 * i + 1, 0, 0)),
                whole(k, nz),
                whole(k, nz),
                column,
                row,
                column,
                row,
            ],
            out_specs=[
                pl.BlockSpec((ROWS, LANES), lambda i, tile: (i, 0)),
                whole(ty, LANES),
                whole(k, nz),
            ],
            scratch_shapes=[
                pltpu.VMEM((nz, 2 * LANES), BF16),
                pltpu.VMEM((ty, LANES), F32),
                pltpu.VMEM((tx, LANES), F32),
                pltpu.VMEM((steps, k, ROWS), F32),
            ],
        ),
        out_shape=[
            jax.ShapeDtypeStruct((tx, LANES), F32),
            jax.ShapeDtypeStruct((ty, LANES), F32),
            jax.ShapeDtypeStruct((k, nz), F32),
        ],
        compiler_params=pltpu.CompilerParams(vmem_limit_bytes=56 << 20),
        cost_estimate=pl.CostEstimate(
            flops=2 * tx * ty * nz * (2 * LANES + k), bytes_accessed=2 * tx * ty * nz, transcendentals=0
        ),
        name="modes",
    )(tile, field, field, z_first.T, z_second.T, y_first.T, x_second.T, y_third.T, x_third.T)


def plane_kernel(targets, place, low, high, other_low, other_high, own, sibling, *refs):
    outs, maps, rows = refs[:-2], refs[-2], refs[-1]

    @pl.when(pl.program_id(0) == 0)
    def _():
        share = maps.shape[0] // targets
        rows[:, :TY] = own[...].astype(F32)
        rows[:, TY:] = sibling[...].astype(F32)
        for j in range(targets):
            here = pl.ds(pl.multiple_of(place[3 + j] * share, 8), share)
            for n in range(2):
                maps[j * share : (j + 1) * share, n * TY : (n + 1) * TY] = rows[here, n * TY : (n + 1) * TY]

    held = maps[...].astype(BF16)
    half = low.shape[0]
    for i in range(0, 2 * half, 2):
        field, other = ((low, other_low), (high, other_high))[i // half]
        pair = [jnp.concatenate([field[k], other[k]], axis=0) for k in (i % half, i % half + 1)]
        result = dot(held, jnp.concatenate(pair, axis=1))
        nz = result.shape[1] // 2
        at = 0
        for out in outs:
            block = result[at : at + out.shape[1]].astype(out.dtype)
            out[i] = block[:, :nz]
            out[i + 1] = block[:, nz:]
            at += out.shape[1]


def plane(place, field, other, y_map, counts):
    tx, ty, nz = field.shape
    targets, size = place.shape[0] - 3, y_map.shape[0]
    low = pl.BlockSpec((ROWS // 2, ty, nz), lambda i, place: (2 * i, 0, 0))
    high = pl.BlockSpec((ROWS // 2, ty, nz), lambda i, place: (2 * i + 1, 0, 0))
    kinds = [(count, BF16) for count in counts] * targets
    return pl.pallas_call(
        functools.partial(plane_kernel, targets),
        grid_spec=pltpu.PrefetchScalarGridSpec(
            num_scalar_prefetch=1,
            grid=(tx // ROWS,),
            in_specs=[
                low,
                high,
                low,
                high,
                pl.BlockSpec((size, ty), lambda i, place: (0, place[1])),
                pl.BlockSpec((size, ty), lambda i, place: (0, place[2])),
            ],
            out_specs=[pl.BlockSpec((ROWS, count, nz), lambda i, place: (i, 0, 0)) for count, _ in kinds],
            scratch_shapes=[
                pltpu.VMEM((targets * sum(counts), 2 * ty), F32),
                pltpu.VMEM((size, 2 * ty), F32),
            ],
        ),
        out_shape=[jax.ShapeDtypeStruct((tx, count, nz), kind) for count, kind in kinds],
        compiler_params=pltpu.CompilerParams(vmem_limit_bytes=56 << 20),
        cost_estimate=pl.CostEstimate(
            flops=4 * tx * ty * nz * targets * sum(counts), bytes_accessed=6 * tx * ty * nz, transcendentals=0
        ),
        name="plane",
    )(place, field, field, other, other, y_map, y_map)


def along_z_kernel(slabs, pack, extras, first, count, near, *refs):
    far, z_map, rows = refs[: -slabs - extras - 2], refs[-slabs - extras - 2], refs[-1]
    added, outs = refs[-slabs - extras - 1 : -slabs - 1], refs[-slabs - 1 : -1]
    tx, _, nz = near.shape
    total = near[...].astype(F32)
    for ref in far:
        total += ref[...].astype(F32)
    total = total[:, first : first + count]
    rows[...] = total.reshape(tx * count, nz)
    width = z_map.shape[1] // slabs
    at = 0
    for g in range(count // pack):
        parts = [rows[pl.ds(g * pack + i, tx, stride=count), :] for i in range(pack)]
        result = dot(jnp.concatenate(parts, axis=1).astype(BF16), z_map[...])
        for t in range(width // LANES):
            for s, out in enumerate(outs):
                block = result[:, s * width + t * LANES : s * width + (t + 1) * LANES]
                out[at : at + tx, :] = block.astype(out.dtype)
            at += tx
    for extra in added:
        for out in outs:
            out[at : at + extra.shape[0], :] = extra[...].astype(out.dtype)
        at += extra.shape[0]


def along_z(near, far, first, count, z_map, slabs, pack, added):
    tx, _, nz = near.shape
    rows = tx * (count // pack) * (z_map.shape[1] // slabs // LANES) + sum(x.shape[0] for x in added)
    return pl.pallas_call(
        functools.partial(along_z_kernel, slabs, pack, len(added), first, count),
        out_shape=[jax.ShapeDtypeStruct((rows, LANES), BF16 if s else F32) for s in range(slabs)],
        scratch_shapes=[pltpu.VMEM((tx * count, nz), F32)],
        compiler_params=pltpu.CompilerParams(vmem_limit_bytes=16 << 20),
        cost_estimate=pl.CostEstimate(
            flops=2 * tx * count // pack * z_map.shape[0] * z_map.shape[1],
            bytes_accessed=8 * tx * count * nz,
            transcendentals=0,
        ),
        name="along_z",
    )(near, *far, z_map, *added)


def along_x_kernel(tall, riders, near, *refs):
    outs = refs[-2 - riders :]
    far, (x_map, *three) = refs[: -4 - 2 * riders + 1], refs[-4 - 2 * riders + 1 : -2 - riders]
    tx = x_map.shape[1]
    piece = x_map.shape[0] // REGIONS

    def total(at, rows):
        found = near[at : at + rows, :]
        for ref in far:
            found += ref[at : at + rows, :].astype(F32)
        return found

    tiles = tall // tx
    for t in range(0, tiles, 2):
        results = [dot(x_map[...], total(at, tx).astype(BF16)) for at in (t * tx, (t + 1) * tx)]
        for r in range(REGIONS):
            block = jnp.concatenate([x[r * piece : (r + 1) * piece] for x in results], axis=0)
            out = outs[r * 2 // REGIONS]
            at = (r % (REGIONS // 2) * tiles + t) * piece
            out[at : at + 2 * piece, :] = block.astype(out.dtype)
    if riders:
        at = REGIONS // 2 * tiles * piece
        outs[2][...] = total(tall, TX)
        two = total(tall + TX, TY)
        for out in outs[:2]:
            out[at : at + TY, :] = two.astype(out.dtype)
            out[at + TY :, :] = three[0][...].astype(out.dtype)


def along_x(near, far, x_map, tall, riders):
    rows = tall // x_map.shape[1] * x_map.shape[0] // 2
    shapes = [(rows, F32), (rows, BF16)]
    if riders:
        rows += TY + riders[0].shape[0]
        shapes = [(rows, F32), (rows, BF16), (TX, F32)]
    return pl.pallas_call(
        functools.partial(along_x_kernel, tall, len(riders)),
        out_shape=[jax.ShapeDtypeStruct((n, LANES), kind) for n, kind in shapes],
        compiler_params=pltpu.CompilerParams(vmem_limit_bytes=16 << 20),
        cost_estimate=pl.CostEstimate(
            flops=2 * tall * x_map.shape[0] * LANES, bytes_accessed=6 * tall * LANES, transcendentals=0
        ),
        name="along_x",
    )(near, *far, x_map, *riders)


def add_split_kernel(half, shared, near, far, *outs):
    for n, out in enumerate(outs[:2]):
        out[:half, :] = (near[n * half : (n + 1) * half, :] + far[n * half : (n + 1) * half, :]).astype(out.dtype)
    rest = near[2 * half :, :] + far[2 * half :, :] if near.shape[0] > 2 * half else None
    if rest is not None and shared:
        for out in outs:
            out[half:, :] = rest.astype(out.dtype)
    elif rest is not None:
        outs[2][...] = rest


def add_split(near, far, half, shared):
    rest = near.shape[0] - 2 * half
    rows = half + rest * shared
    shapes = [(rows, F32), (rows, BF16)] + ([(rest, F32)] if rest and not shared else [])
    return pl.pallas_call(
        functools.partial(add_split_kernel, half, shared),
        out_shape=[jax.ShapeDtypeStruct((n, LANES), kind) for n, kind in shapes],
        compiler_params=pltpu.CompilerParams(vmem_limit_bytes=16 << 20),
        cost_estimate=pl.CostEstimate(
            flops=near.size, bytes_accessed=9 * near.size, transcendentals=0
        ),
        name="add_split",
    )(near, far)


def unpack_kernel(counts, pack, width, columns, column, sketches, *refs):
    groups, modes, out, rows, flat = refs[: len(counts)], refs[-6:-3], refs[-3], refs[-2], refs[-1]
    p_rows, s_size, z_size = out.shape
    at = 0
    for mode in modes:
        height, wide = mode.shape
        mode[...] = sketches[pl.ds(at + column[0] * height, height), :][:, :wide]
        at += columns * height
    low = columns // 2
    half = low * p_rows
    first = 0
    for pieces, group in zip(groups, counts):
        size = pieces.shape[0] // columns
        rows[: pieces.shape[0], :] = pieces[...].astype(F32)
        for d in range(columns):
            source = (reverse_bits(d % low, low) * 2 + d // low) * size
            q = first
            for count in group:
                for g in range(count // pack):
                    wide = jnp.concatenate(
                        [
                            rows[source + t * half : source + (t + 1) * half, :]
                            for t in range(width // LANES)
                        ],
                        axis=1,
                    )
                    source += half * (width // LANES)
                    for i in range(pack):
                        at = (g * pack + i) * half
                        flat[at : at + half, :z_size] = wide[:, i * z_size : (i + 1) * z_size]
                start = pl.multiple_of((column[0] ^ d) * (s_size // columns) + q, UNIT)
                for p in range(p_rows):
                    found = flat[pl.ds(d % low * p_rows + p, count, stride=half), :]
                    out[p, pl.ds(start, count), :] = found[:, :z_size]
                q += count
        first += sum(group)


def unpack(groups, counts, sketches, column, shapes, sizes):
    pack, width, columns = sizes
    half = columns // 2 * shapes[-1][0]
    vmem = pl.BlockSpec(memory_space=pltpu.VMEM)
    return pl.pallas_call(
        functools.partial(unpack_kernel, counts, pack, width, columns),
        in_specs=[pl.BlockSpec(memory_space=pltpu.SMEM)] + [vmem] * (1 + len(groups)),
        out_specs=[vmem] * len(shapes),
        out_shape=[jax.ShapeDtypeStruct(shape, F32) for shape in shapes],
        scratch_shapes=[
            pltpu.VMEM((max(x.shape[0] for x in groups), LANES), F32),
            pltpu.VMEM((max(sum(counts, [])) * half, LANES), F32),
        ],
        compiler_params=pltpu.CompilerParams(vmem_limit_bytes=16 << 20),
        cost_estimate=pl.CostEstimate(
            flops=4 * groups[0].size, bytes_accessed=8 * groups[0].size, transcendentals=0
        ),
        name="unpack",
    )(column.reshape(1).astype(jnp.int32), sketches, *groups)


def reverse_bits(value, size):
    bits = size.bit_length() - 1
    return sum(((value >> n) & 1) << (bits - 1 - n) for n in range(bits))


def after(token, *values):
    return lax.optimization_barrier((token, *values))[1:]


def shards(
    field_tiles, core_x, core_y, core_z, x_second, x_third, y_first, y_third, z_first, z_second
):
    tiles, slabs = lax.axis_size("xy"), lax.axis_size("gz")
    row_tiles = core_x.shape[0] // TX
    column_tiles = tiles // row_tiles
    pairs = column_tiles // 2
    me, slab = lax.axis_index("xy"), lax.axis_index("gz")
    u, v = me // column_tiles, me % column_tiles
    side, pair = v % 2, v // 2
    s_size, k = core_x.shape[1], x_third.shape[1]
    field = field_tiles[0]
    nz = field.shape[2]
    share = s_size // column_tiles
    units = share // UNIT
    counts = [UNIT * n for n in (PLAN if sum(PLAN) == units else [1] * units)]
    chunks = len(counts)
    riding = min(RIDING, chunks - 1)
    groups = PAIR_PLAN if sum(PAIR_PLAN) == chunks else [1] * chunks
    place = [(g, n) for g, size in enumerate(groups) for n in range(size)]
    starts = [sum(counts[c - n : c]) for c, (_, n) in enumerate(place)]
    wides = [sum(counts[c] for c in range(chunks) if place[c][0] == g) for g in range(len(groups))]
    early = min(max(EARLY, riding + 1), chunks - 1)
    z_size = s_size // slabs
    p_size = s_size // row_tiles
    p_rows = s_size // tiles
    pack = PACK if PACK * z_size % LANES == 0 else UNIT
    width = -(-pack * z_size // LANES) * LANES
    one_rows = core_x.shape[0] // (tiles * slabs)
    two_rows = core_y.shape[0] // (tiles * slabs)
    three_rows = k // tiles

    def flip(x, bit):
        return lax.ppermute(x, "xy", [(i, i ^ bit) for i in range(tiles)])

    def to_pair(x, step):
        def target(i):
            row, column = divmod(i, column_tiles)
            return row * column_tiles + (column // 2 + step) % pairs * 2 + column % 2

        return lax.ppermute(x, "xy", [(i, target(i)) for i in range(tiles)])

    def to_slab(x, step):
        if step == 0:
            return x
        return lax.ppermute(x, "gz", [(i, (i + step) % slabs) for i in range(slabs)])

    other = flip(field, 1)
    owners = [(pair + j) % pairs * 2 + side for j in range(pairs)]
    columns = jnp.stack([u, v, v + 1 - 2 * side, *owners]).astype(jnp.int32)
    one, two, three = modes(columns, field, z_first, z_second, y_first, x_second, y_third, x_third)
    (columns,) = after(one, columns)
    parts = plane(columns, field, other, core_y.T, wides)
    core_x, core_z = after(parts[0], core_x, core_z)
    arrived = [
        [to_pair(parts[j * len(wides) + g], j) for j in range(1, pairs)] for g in range(len(wides))
    ]

    z_map = []
    for step in range(slabs):
        block = cut(core_z, (slab + step) % slabs * z_size, z_size, 1)
        block = jnp.eye(pack, dtype=BF16)[:, None, :, None] * block[None, :, None, :]
        block = block.reshape(pack * nz, pack * z_size)
        z_map.append(jnp.pad(block, ((0, 0), (0, width - pack * z_size))))
    z_map = jnp.concatenate(z_map, axis=1)
    order = sorted(range(row_tiles), key=lambda j: (j % 2, j))
    at = jnp.arange(s_size, dtype=jnp.int32)
    far = jnp.array(order, jnp.int32)[at // p_size]
    wanted = ((u ^ far) * column_tiles + (v ^ (at % p_size // p_rows))) * p_rows + at % p_rows
    chosen = (wanted[:, None] == at[None, :]).astype(BF16)
    x_map = dot(chosen, cut(core_x.T, u * TX, TX, 1)).astype(BF16)

    tiles_wide = [count // pack * (width // LANES) for count in counts]
    slabbed, mixed, sums, blocks = {}, {}, {}, {}
    small = []

    def end_y(c, token):
        added = []
        if c == riding:
            added = [one, two]
        group = place[c][0]
        near, *far = after(token, parts[group], *arrived[group])
        near, *send = along_z(near, far, starts[c], counts[c], z_map, slabs, pack, added)
        slabbed[c] = [near] + [to_slab(x, step + 1) for step, x in enumerate(send)]
        return send[0]

    def end_z(c, token):
        tall = TX * tiles_wide[c]
        near, *far = after(token, *slabbed[c])
        keep, send, *rest = along_x(near, far, x_map, tall, [three] if c == riding else [])
        small.extend(rest)
        mixed[c] = (keep, flip(send, column_tiles))
        return send

    def add_near(c, token):
        keep, got = after(token, *mixed[c])
        mine, send = add_split(keep, got, p_size * tiles_wide[c], True)
        sums[c] = (mine, flip(send, 2 * column_tiles))
        return send

    def add_far(c, token):
        mine, got = after(token, *sums[c])
        near, away, *rest = add_split(mine, got, p_size // 2 * tiles_wide[c], False)
        small.extend(rest)
        blocks[c] = (near, away)
        return away

    def exchange(group, sketches):
        near = jnp.concatenate([blocks[c][0].astype(BF16) for c in group], axis=0)
        rows = near.shape[0]
        sent = [blocks[c][1] for c in group]
        if sketches is not None:
            sent.append(sketches.astype(BF16))
        got = flip(jnp.concatenate(sent, axis=0), column_tiles // 2)
        if sketches is not None:
            sketches = sketches + got[rows:].astype(F32)
        pieces = jnp.concatenate([near, got[:rows]], axis=0)
        bit = column_tiles // 4
        while bit:
            size = pieces.shape[0]
            sent = pieces
            if sketches is not None:
                sent = jnp.concatenate([pieces, sketches.astype(BF16)], axis=0)
            got = flip(sent, bit)
            if sketches is not None:
                sketches = sketches + got[size:].astype(F32)
            pieces = jnp.concatenate([pieces, got[:size]], axis=0)
            bit //= 2
        return pieces, sketches

    def sketch_rows():
        slab_cut = lambda x, rows: lax.dynamic_index_in_dim(
            x.reshape(-1, slabs, rows, LANES), slab, 1, False
        ).reshape(-1, LANES)
        mine = slab_cut(small[0][:TX], one_rows)
        theirs = slab_cut(small[1][:TY], two_rows)
        turns = column_tiles // row_tiles
        theirs = jnp.concatenate([jnp.where(v == u * turns + n, theirs, 0.0) for n in range(turns)])
        last = cut(small[1][TY:], u * (k // row_tiles), k // row_tiles, 0)
        return jnp.concatenate([mine, theirs, last], axis=0)

    stages = [end_y, end_z, add_near, add_far]
    begun = [2 * sum(counts[:c]) / UNIT for c in range(chunks)]
    order = sorted((begun[c] + LAG * n, n, c) for c in range(chunks) for n in range(len(stages)))
    token, ends = parts[0], -1
    for at, (_, n, c) in enumerate(order):
        if at == ends:
            token = first
        token = stages[n](c, token)
        if stages[n] is add_far and c == early - 1:
            first, sketches = exchange(range(early), sketch_rows())
            ends = at + WAIT if WAIT else -1
    last, _ = exchange(range(early, chunks), None)
    mode_one, mode_two, mode_three, core_sketch = unpack(
        [first, last],
        [counts[:early], counts[early:]],
        sketches,
        v,
        [(one_rows, k), (two_rows, k), (three_rows, nz), (p_rows, s_size, z_size)],
        (pack, width, column_tiles),
    )
    return mode_one, mode_two, mode_three, core_sketch


def solution(mesh):
    return jax.shard_map(
        shards,
        mesh=mesh,
        in_specs=(
            P("xy", None, None, "gz"),
            P(),
            P(),
            P("gz", None),
            P(),
            P(),
            P(),
            P(),
            P("gz", None),
            P("gz", None),
        ),
        out_specs=(
            P(("xy", "gz"), None),
            P(("xy", "gz"), None),
            P("xy", "gz"),
            P("xy", None, "gz"),
        ),
        check_vma=False,
    )
```

```python
import functools

import jax
import jax.numpy as jnp
from jax import lax
from jax.experimental import pallas as pl
from jax.experimental.pallas import tpu as pltpu
from jax.sharding import PartitionSpec as P

TX = 128
TY = 128
LANES = 128
REGIONS = 8
ROWS = 32
UNIT = 8
PLAN = (1, 1, 1, 1, 1, 1)
PAIR_PLAN = (1, 1, 1, 1, 1, 1)
RIDING = 1
EARLY = 4
WAIT = 0
LAG = 3.1
PACK = 4
F32 = jnp.float32
BF16 = jnp.bfloat16


def dot(a, b):
    return jnp.dot(a, b, preferred_element_type=F32)


def cut(matrix, offset, length, axis):
    return lax.dynamic_slice_in_dim(matrix, offset, length, axis)


def modes_kernel(
    tile, low, high, z_first, z_second, y_one, x_two, y_three, x_three, one, two, three, z_pair, ones, twos, x_parts
):
    del tile
    step, rows = pl.program_id(0), 2 * low.shape[0]
    k = y_three.shape[0]

    @pl.when(step == 0)
    def _():
        two[...] = jnp.zeros_like(two)
        three[...] = jnp.zeros_like(three)
        for ref in (z_pair, ones, twos):
            ref[...] = jnp.zeros_like(ref)
        z_pair[:, :k] = z_first[...].astype(F32).T.astype(BF16)
        z_pair[:, LANES : LANES + k] = z_second[...].astype(F32).T.astype(BF16)
        ones[:, :k] = y_one[...].astype(F32).T
        twos[:, :k] = x_two[...].astype(F32).T
        for n in range(x_parts.shape[0]):
            x_parts[n] = x_three[...].astype(F32)[:, n * rows : (n + 1) * rows]

    sum_two = jnp.zeros(two.shape, F32)
    sum_three = jnp.zeros(three.shape, F32)
    for i in range(rows):
        plane = (low, high)[i * 2 // rows][i % low.shape[0]]
        paired = dot(plane, z_pair[...])
        one[i : i + 1, :] = jnp.sum(paired[:, :LANES] * ones[...], axis=0, keepdims=True)
        sum_two += paired[:, LANES:] * twos[pl.ds(step * rows + i, 1), :]
        sum_three += dot(y_three[...], plane) * x_parts[step, :, i : i + 1]
    two[...] += sum_two
    three[...] += sum_three


def modes(tile, field, z_first, z_second, y_first, x_second, y_third, x_third):
    tx, ty, nz = field.shape
    k = z_first.shape[1]
    steps = tx // ROWS
    whole = lambda *shape: pl.BlockSpec(shape, lambda i, tile: (0,) * len(shape))
    row = pl.BlockSpec((k, tx), lambda i, tile: (0, tile[0]))
    column = pl.BlockSpec((k, ty), lambda i, tile: (0, tile[1]))
    return pl.pallas_call(
        modes_kernel,
        grid_spec=pltpu.PrefetchScalarGridSpec(
            num_scalar_prefetch=1,
            grid=(steps,),
            in_specs=[
                pl.BlockSpec((ROWS // 2, ty, nz), lambda i, tile: (2 * i, 0, 0)),
                pl.BlockSpec((ROWS // 2, ty, nz), lambda i, tile: (2 * i + 1, 0, 0)),
                whole(k, nz),
                whole(k, nz),
                column,
                row,
                column,
                row,
            ],
            out_specs=[
                pl.BlockSpec((ROWS, LANES), lambda i, tile: (i, 0)),
                whole(ty, LANES),
                whole(k, nz),
            ],
            scratch_shapes=[
                pltpu.VMEM((nz, 2 * LANES), BF16),
                pltpu.VMEM((ty, LANES), F32),
                pltpu.VMEM((tx, LANES), F32),
                pltpu.VMEM((steps, k, ROWS), F32),
            ],
        ),
        out_shape=[
            jax.ShapeDtypeStruct((tx, LANES), F32),
            jax.ShapeDtypeStruct((ty, LANES), F32),
            jax.ShapeDtypeStruct((k, nz), F32),
        ],
        compiler_params=pltpu.CompilerParams(vmem_limit_bytes=56 << 20),
        cost_estimate=pl.CostEstimate(
            flops=2 * tx * ty * nz * (2 * LANES + k), bytes_accessed=2 * tx * ty * nz, transcendentals=0
        ),
        name="modes",
    )(tile, field, field, z_first.T, z_second.T, y_first.T, x_second.T, y_third.T, x_third.T)


def plane_kernel(targets, place, low, high, other_low, other_high, own, sibling, *refs):
    outs, maps, rows = refs[:-2], refs[-2], refs[-1]

    @pl.when(pl.program_id(0) == 0)
    def _():
        share = maps.shape[0] // targets
        rows[:, :TY] = own[...].astype(F32)
        rows[:, TY:] = sibling[...].astype(F32)
        for j in range(targets):
            here = pl.ds(pl.multiple_of(place[3 + j] * share, 8), share)
            for n in range(2):
                maps[j * share : (j + 1) * share, n * TY : (n + 1) * TY] = rows[here, n * TY : (n + 1) * TY]

    held = maps[...].astype(BF16)
    half = low.shape[0]
    for i in range(0, 2 * half, 2):
        field, other = ((low, other_low), (high, other_high))[i // half]
        pair = [jnp.concatenate([field[k], other[k]], axis=0) for k in (i % half, i % half + 1)]
        result = dot(held, jnp.concatenate(pair, axis=1))
        nz = result.shape[1] // 2
        at = 0
        for out in outs:
            block = result[at : at + out.shape[1]].astype(out.dtype)
            out[i] = block[:, :nz]
            out[i + 1] = block[:, nz:]
            at += out.shape[1]


def plane(place, field, other, y_map, counts):
    tx, ty, nz = field.shape
    targets, size = place.shape[0] - 3, y_map.shape[0]
    low = pl.BlockSpec((ROWS // 2, ty, nz), lambda i, place: (2 * i, 0, 0))
    high = pl.BlockSpec((ROWS // 2, ty, nz), lambda i, place: (2 * i + 1, 0, 0))
    kinds = [(count, BF16) for count in counts] * targets
    return pl.pallas_call(
        functools.partial(plane_kernel, targets),
        grid_spec=pltpu.PrefetchScalarGridSpec(
            num_scalar_prefetch=1,
            grid=(tx // ROWS,),
            in_specs=[
                low,
                high,
                low,
                high,
                pl.BlockSpec((size, ty), lambda i, place: (0, place[1])),
                pl.BlockSpec((size, ty), lambda i, place: (0, place[2])),
            ],
            out_specs=[pl.BlockSpec((ROWS, count, nz), lambda i, place: (i, 0, 0)) for count, _ in kinds],
            scratch_shapes=[
                pltpu.VMEM((targets * sum(counts), 2 * ty), F32),
                pltpu.VMEM((size, 2 * ty), F32),
            ],
        ),
        out_shape=[jax.ShapeDtypeStruct((tx, count, nz), kind) for count, kind in kinds],
        compiler_params=pltpu.CompilerParams(vmem_limit_bytes=56 << 20),
        cost_estimate=pl.CostEstimate(
            flops=4 * tx * ty * nz * targets * sum(counts), bytes_accessed=6 * tx * ty * nz, transcendentals=0
        ),
        name="plane",
    )(place, field, field, other, other, y_map, y_map)


def along_z_kernel(slabs, pack, extras, first, count, near, *refs):
    far, z_map, rows = refs[: -slabs - extras - 2], refs[-slabs - extras - 2], refs[-1]
    added, outs = refs[-slabs - extras - 1 : -slabs - 1], refs[-slabs - 1 : -1]
    tx, _, nz = near.shape
    total = near[...].astype(F32)
    for ref in far:
        total += ref[...].astype(F32)
    total = total[:, first : first + count]
    rows[...] = total.reshape(tx * count, nz)
    width = z_map.shape[1] // slabs
    at = 0
    for g in range(count // pack):
        parts = [rows[pl.ds(g * pack + i, tx, stride=count), :] for i in range(pack)]
        result = dot(jnp.concatenate(parts, axis=1).astype(BF16), z_map[...])
        for t in range(width // LANES):
            for s, out in enumerate(outs):
                block = result[:, s * width + t * LANES : s * width + (t + 1) * LANES]
                out[at : at + tx, :] = block.astype(out.dtype)
            at += tx
    for extra in added:
        for out in outs:
            out[at : at + extra.shape[0], :] = extra[...].astype(out.dtype)
        at += extra.shape[0]


def along_z(near, far, first, count, z_map, slabs, pack, added):
    tx, _, nz = near.shape
    rows = tx * (count // pack) * (z_map.shape[1] // slabs // LANES) + sum(x.shape[0] for x in added)
    return pl.pallas_call(
        functools.partial(along_z_kernel, slabs, pack, len(added), first, count),
        out_shape=[jax.ShapeDtypeStruct((rows, LANES), BF16 if s else F32) for s in range(slabs)],
        scratch_shapes=[pltpu.VMEM((tx * count, nz), F32)],
        compiler_params=pltpu.CompilerParams(vmem_limit_bytes=16 << 20),
        cost_estimate=pl.CostEstimate(
            flops=2 * tx * count // pack * z_map.shape[0] * z_map.shape[1],
            bytes_accessed=8 * tx * count * nz,
            transcendentals=0,
        ),
        name="along_z",
    )(near, *far, z_map, *added)


def along_x_kernel(tall, riders, near, *refs):
    outs = refs[-2 - riders :]
    far, (x_map, *three) = refs[: -4 - 2 * riders + 1], refs[-4 - 2 * riders + 1 : -2 - riders]
    tx = x_map.shape[1]
    piece = x_map.shape[0] // REGIONS

    def total(at, rows):
        found = near[at : at + rows, :]
        for ref in far:
            found += ref[at : at + rows, :].astype(F32)
        return found

    tiles = tall // tx
    for t in range(0, tiles, 2):
        results = [dot(x_map[...], total(at, tx).astype(BF16)) for at in (t * tx, (t + 1) * tx)]
        for r in range(REGIONS):
            block = jnp.concatenate([x[r * piece : (r + 1) * piece] for x in results], axis=0)
            out = outs[r * 2 // REGIONS]
            at = (r % (REGIONS // 2) * tiles + t) * piece
            out[at : at + 2 * piece, :] = block.astype(out.dtype)
    if riders:
        at = REGIONS // 2 * tiles * piece
        outs[2][...] = total(tall, TX)
        two = total(tall + TX, TY)
        for out in outs[:2]:
            out[at : at + TY, :] = two.astype(out.dtype)
            out[at + TY :, :] = three[0][...].astype(out.dtype)


def along_x(near, far, x_map, tall, riders):
    rows = tall // x_map.shape[1] * x_map.shape[0] // 2
    shapes = [(rows, F32), (rows, BF16)]
    if riders:
        rows += TY + riders[0].shape[0]
        shapes = [(rows, F32), (rows, BF16), (TX, F32)]
    return pl.pallas_call(
        functools.partial(along_x_kernel, tall, len(riders)),
        out_shape=[jax.ShapeDtypeStruct((n, LANES), kind) for n, kind in shapes],
        compiler_params=pltpu.CompilerParams(vmem_limit_bytes=16 << 20),
        cost_estimate=pl.CostEstimate(
            flops=2 * tall * x_map.shape[0] * LANES, bytes_accessed=6 * tall * LANES, transcendentals=0
        ),
        name="along_x",
    )(near, *far, x_map, *riders)


def add_split_kernel(half, shared, near, far, *outs):
    for n, out in enumerate(outs[:2]):
        out[:half, :] = (near[n * half : (n + 1) * half, :] + far[n * half : (n + 1) * half, :]).astype(out.dtype)
    rest = near[2 * half :, :] + far[2 * half :, :] if near.shape[0] > 2 * half else None
    if rest is not None and shared:
        for out in outs:
            out[half:, :] = rest.astype(out.dtype)
    elif rest is not None:
        outs[2][...] = rest


def add_split(near, far, half, shared):
    rest = near.shape[0] - 2 * half
    rows = half + rest * shared
    shapes = [(rows, F32), (rows, BF16)] + ([(rest, F32)] if rest and not shared else [])
    return pl.pallas_call(
        functools.partial(add_split_kernel, half, shared),
        out_shape=[jax.ShapeDtypeStruct((n, LANES), kind) for n, kind in shapes],
        compiler_params=pltpu.CompilerParams(vmem_limit_bytes=16 << 20),
        cost_estimate=pl.CostEstimate(
            flops=near.size, bytes_accessed=9 * near.size, transcendentals=0
        ),
        name="add_split",
    )(near, far)


def unpack_kernel(counts, pack, width, columns, column, sketches, *refs):
    groups, modes, out, rows, flat = refs[: len(counts)], refs[-6:-3], refs[-3], refs[-2], refs[-1]
    p_rows, s_size, z_size = out.shape
    at = 0
    for mode in modes:
        height, wide = mode.shape
        mode[...] = sketches[pl.ds(at + column[0] * height, height), :][:, :wide]
        at += columns * height
    low = columns // 2
    half = low * p_rows
    first = 0
    for pieces, group in zip(groups, counts):
        size = pieces.shape[0] // columns
        rows[: pieces.shape[0], :] = pieces[...].astype(F32)
        for d in range(columns):
            source = (reverse_bits(d % low, low) * 2 + d // low) * size
            q = first
            for count in group:
                for g in range(count // pack):
                    wide = jnp.concatenate(
                        [
                            rows[source + t * half : source + (t + 1) * half, :]
                            for t in range(width // LANES)
                        ],
                        axis=1,
                    )
                    source += half * (width // LANES)
                    for i in range(pack):
                        at = (g * pack + i) * half
                        flat[at : at + half, :z_size] = wide[:, i * z_size : (i + 1) * z_size]
                start = pl.multiple_of((column[0] ^ d) * (s_size // columns) + q, UNIT)
                for p in range(p_rows):
                    found = flat[pl.ds(d % low * p_rows + p, count, stride=half), :]
                    out[p, pl.ds(start, count), :] = found[:, :z_size]
                q += count
        first += sum(group)


def unpack(groups, counts, sketches, column, shapes, sizes):
    pack, width, columns = sizes
    half = columns // 2 * shapes[-1][0]
    vmem = pl.BlockSpec(memory_space=pltpu.VMEM)
    return pl.pallas_call(
        functools.partial(unpack_kernel, counts, pack, width, columns),
        in_specs=[pl.BlockSpec(memory_space=pltpu.SMEM)] + [vmem] * (1 + len(groups)),
        out_specs=[vmem] * len(shapes),
        out_shape=[jax.ShapeDtypeStruct(shape, F32) for shape in shapes],
        scratch_shapes=[
            pltpu.VMEM((max(x.shape[0] for x in groups), LANES), F32),
            pltpu.VMEM((max(sum(counts, [])) * half, LANES), F32),
        ],
        compiler_params=pltpu.CompilerParams(vmem_limit_bytes=16 << 20),
        cost_estimate=pl.CostEstimate(
            flops=4 * groups[0].size, bytes_accessed=8 * groups[0].size, transcendentals=0
        ),
        name="unpack",
    )(column.reshape(1).astype(jnp.int32), sketches, *groups)


def reverse_bits(value, size):
    bits = size.bit_length() - 1
    return sum(((value >> n) & 1) << (bits - 1 - n) for n in range(bits))


def after(token, *values):
    return lax.optimization_barrier((token, *values))[1:]


def shards(
    field_tiles, core_x, core_y, core_z, x_second, x_third, y_first, y_third, z_first, z_second
):
    tiles, slabs = lax.axis_size("xy"), lax.axis_size("gz")
    row_tiles = core_x.shape[0] // TX
    column_tiles = tiles // row_tiles
    pairs = column_tiles // 2
    me, slab = lax.axis_index("xy"), lax.axis_index("gz")
    u, v = me // column_tiles, me % column_tiles
    side, pair = v % 2, v // 2
    s_size, k = core_x.shape[1], x_third.shape[1]
    field = field_tiles[0]
    nz = field.shape[2]
    share = s_size // column_tiles
    units = share // UNIT
    counts = [UNIT * n for n in (PLAN if sum(PLAN) == units else [1] * units)]
    chunks = len(counts)
    riding = min(RIDING, chunks - 1)
    groups = PAIR_PLAN if sum(PAIR_PLAN) == chunks else [1] * chunks
    place = [(g, n) for g, size in enumerate(groups) for n in range(size)]
    starts = [sum(counts[c - n : c]) for c, (_, n) in enumerate(place)]
    wides = [sum(counts[c] for c in range(chunks) if place[c][0] == g) for g in range(len(groups))]
    early = min(max(EARLY, riding + 1), chunks - 1)
    z_size = s_size // slabs
    p_size = s_size // row_tiles
    p_rows = s_size // tiles
    pack = PACK if PACK * z_size % LANES == 0 else UNIT
    width = -(-pack * z_size // LANES) * LANES
    one_rows = core_x.shape[0] // (tiles * slabs)
    two_rows = core_y.shape[0] // (tiles * slabs)
    three_rows = k // tiles

    def flip(x, bit):
        return lax.ppermute(x, "xy", [(i, i ^ bit) for i in range(tiles)])

    def to_pair(x, step):
        def target(i):
            row, column = divmod(i, column_tiles)
            return row * column_tiles + (column // 2 + step) % pairs * 2 + column % 2

        return lax.ppermute(x, "xy", [(i, target(i)) for i in range(tiles)])

    def to_slab(x, step):
        if step == 0:
            return x
        return lax.ppermute(x, "gz", [(i, (i + step) % slabs) for i in range(slabs)])

    other = flip(field, 1)
    owners = [(pair + j) % pairs * 2 + side for j in range(pairs)]
    columns = jnp.stack([u, v, v + 1 - 2 * side, *owners]).astype(jnp.int32)
    one, two, three = modes(columns, field, z_first, z_second, y_first, x_second, y_third, x_third)
    (columns,) = after(one, columns)
    parts = plane(columns, field, other, core_y.T, wides)
    core_x, core_z = after(parts[0], core_x, core_z)
    arrived = [
        [to_pair(parts[j * len(wides) + g], j) for j in range(1, pairs)] for g in range(len(wides))
    ]

    z_map = []
    for step in range(slabs):
        block = cut(core_z, (slab + step) % slabs * z_size, z_size, 1)
        block = jnp.eye(pack, dtype=BF16)[:, None, :, None] * block[None, :, None, :]
        block = block.reshape(pack * nz, pack * z_size)
        z_map.append(jnp.pad(block, ((0, 0), (0, width - pack * z_size))))
    z_map = jnp.concatenate(z_map, axis=1)
    order = sorted(range(row_tiles), key=lambda j: (j % 2, j))
    at = jnp.arange(s_size, dtype=jnp.int32)
    far = jnp.array(order, jnp.int32)[at // p_size]
    wanted = ((u ^ far) * column_tiles + (v ^ (at % p_size // p_rows))) * p_rows + at % p_rows
    chosen = (wanted[:, None] == at[None, :]).astype(BF16)
    x_map = dot(chosen, cut(core_x.T, u * TX, TX, 1)).astype(BF16)

    tiles_wide = [count // pack * (width // LANES) for count in counts]
    slabbed, mixed, sums, blocks = {}, {}, {}, {}
    small = []

    def end_y(c, token):
        added = []
        if c == riding:
            added = [one, two]
        group = place[c][0]
        near, *far = after(token, parts[group], *arrived[group])
        near, *send = along_z(near, far, starts[c], counts[c], z_map, slabs, pack, added)
        slabbed[c] = [near] + [to_slab(x, step + 1) for step, x in enumerate(send)]
        return send[0]

    def end_z(c, token):
        tall = TX * tiles_wide[c]
        near, *far = after(token, *slabbed[c])
        keep, send, *rest = along_x(near, far, x_map, tall, [three] if c == riding else [])
        small.extend(rest)
        mixed[c] = (keep, flip(send, column_tiles))
        return send

    def add_near(c, token):
        keep, got = after(token, *mixed[c])
        mine, send = add_split(keep, got, p_size * tiles_wide[c], True)
        sums[c] = (mine, flip(send, 2 * column_tiles))
        return send

    def add_far(c, token):
        mine, got = after(token, *sums[c])
        near, away, *rest = add_split(mine, got, p_size // 2 * tiles_wide[c], False)
        small.extend(rest)
        blocks[c] = (near, away)
        return away

    def exchange(group, sketches):
        near = jnp.concatenate([blocks[c][0].astype(BF16) for c in group], axis=0)
        rows = near.shape[0]
        sent = [blocks[c][1] for c in group]
        if sketches is not None:
            sent.append(sketches.astype(BF16))
        got = flip(jnp.concatenate(sent, axis=0), column_tiles // 2)
        if sketches is not None:
            sketches = sketches + got[rows:].astype(F32)
        pieces = jnp.concatenate([near, got[:rows]], axis=0)
        bit = column_tiles // 4
        while bit:
            size = pieces.shape[0]
            sent = pieces
            if sketches is not None:
                sent = jnp.concatenate([pieces, sketches.astype(BF16)], axis=0)
            got = flip(sent, bit)
            if sketches is not None:
                sketches = sketches + got[size:].astype(F32)
            pieces = jnp.concatenate([pieces, got[:size]], axis=0)
            bit //= 2
        return pieces, sketches

    def sketch_rows():
        slab_cut = lambda x, rows: lax.dynamic_index_in_dim(
            x.reshape(-1, slabs, rows, LANES), slab, 1, False
        ).reshape(-1, LANES)
        mine = slab_cut(small[0][:TX], one_rows)
        theirs = slab_cut(small[1][:TY], two_rows)
        turns = column_tiles // row_tiles
        theirs = jnp.concatenate([jnp.where(v == u * turns + n, theirs, 0.0) for n in range(turns)])
        last = cut(small[1][TY:], u * (k // row_tiles), k // row_tiles, 0)
        return jnp.concatenate([mine, theirs, last], axis=0)

    stages = [end_y, end_z, add_near, add_far]
    begun = [2 * sum(counts[:c]) / UNIT for c in range(chunks)]
    order = sorted((begun[c] + LAG * n, n, c) for c in range(chunks) for n in range(len(stages)))
    token, ends = parts[0], -1
    for at, (_, n, c) in enumerate(order):
        if at == ends:
            token = first
        token = stages[n](c, token)
        if stages[n] is add_far and c == early - 1:
            first, sketches = exchange(range(early), sketch_rows())
            ends = at + WAIT if WAIT else -1
    last, _ = exchange(range(early, chunks), None)
    mode_one, mode_two, mode_three, core_sketch = unpack(
        [first, last],
        [counts[:early], counts[early:]],
        sketches,
        v,
        [(one_rows, k), (two_rows, k), (three_rows, nz), (p_rows, s_size, z_size)],
        (pack, width, column_tiles),
    )
    return mode_one, mode_two, mode_three, core_sketch


def solution(mesh):
    return jax.shard_map(
        shards,
        mesh=mesh,
        in_specs=(
            P("xy", None, None, "gz"),
            P(),
            P(),
            P("gz", None),
            P(),
            P(),
            P(),
            P(),
            P("gz", None),
            P("gz", None),
        ),
        out_specs=(
            P(("xy", "gz"), None),
            P(("xy", "gz"), None),
            P("xy", "gz"),
            P("xy", None, "gz"),
        ),
        check_vma=False,
    )
```
